256 devices in a mesh: dp: 32 (over z, y_hi, core), tensor: 8 (over y_lo, x).
Axes of the slice: x: 4, y: 4 (y_hi: 2, y_lo: 2; y = y_hi * 2 + y_lo), z: 8, core: 2. Of those that a mesh axis runs over, the one named last changes fastest.
Arguments:
- image_feat: bfloat16 [16384, 1152], P('dp', 'tensor'), as said below
- text_feat: bfloat16 [16384, 1152], P('dp', 'tensor'), as said below
- image_head: bfloat16 [1152, 1152], P('tensor'), may hold values from -0.1875 to 0.1875
- text_head: bfloat16 [1152, 1152], P('tensor'), may hold values from -0.1875 to 0.1875
- logit_scale: float32 [1], replicated, may hold values from 4 to 12
- logit_bias: float32 [1], replicated, may hold values from -4 to -1
Outputs:
- grad_image_head: float32 [1152, 1152], P('tensor')
- grad_text_head: float32 [1152, 1152], P('tensor')
- row_loss: float32 [16384], P('dp')
The draws below stay inside these ranges and needn't reach their ends.
Inputs may be any that keep to these rules, and one draw needn't show every extreme that they name: `image_feat`: feature rows and columns have different scales. `text_feat`: feature rows and columns have different scales.
All inputs are finite; a program needn't handle non-finite values.
Results may differ from the reference program's by a relative error of at most 0.0065.
Values may be sent and summed in bfloat16 or wider, within the bound.
No kernel may reach another device: no remote copies, remote signals or barrier semaphores. Data moves between devices by JAX's collectives and lax.ppermute only.
A program may use at most 64 MiB of HBM per device.

```python
import math
import jax
import jax.numpy as jnp
from jax import lax

D = 1152
E = 1152
PAIRS_DEV = 512
BATCH = 16384


def feature_draw(key):
    key_main, key_rows, key_cols = jax.random.split(key, 3)
    base = jax.random.normal(key_main, (BATCH, D), jnp.float32)
    row_scale = jnp.exp(jax.random.uniform(key_rows, (BATCH, 1), jnp.float32, 0.0, math.log(10.0)))
    col_scale = jnp.exp(jax.random.uniform(key_cols, (1, D), jnp.float32, math.log(0.5), math.log(2.0)))
    return (base * row_scale * col_scale).astype(jnp.bfloat16)


def draw_image_feat(key, part):
    key = jax.random.fold_in(key, 11)
    return feature_draw(key)


def draw_text_feat(key, part):
    key = jax.random.fold_in(key, 12)
    return feature_draw(key)


def level_of(rng, extent, shards, least, high):
    loudness = 1.0
    for position, parts in shards:
        steps = jax.random.uniform(jax.random.fold_in(jax.random.fold_in(rng, 6), position), (parts,), jnp.float32, least / len(shards), high / len(shards))
        loudness = loudness * jnp.repeat(jnp.exp(steps), extent[position] // parts).reshape((-1,) + (1,) * (len(extent) - 1 - position))
    return loudness


def centred(key, shape, deviation, reach, shards=(), held_as=jnp.bfloat16):
    entries = jax.random.normal(key, shape, jnp.float32) * deviation
    if len(shards) > 0:
        entries = level_of(key, shape, shards, -0.22, 0.18) * entries
    return jnp.clip(entries, min=-reach, max=reach).astype(held_as)


def setup_inputs(seed: int = 0) -> dict:
    splits = jax.random.split(jax.random.key(seed), 7)
    return {
        "image_feat": draw_image_feat(jax.random.fold_in(splits[6], 71), 0),
        "text_feat": draw_text_feat(jax.random.fold_in(splits[6], 71), 0),
        "image_head": centred(splits[2], (D, E), D ** -0.5, 0.1875, ((0, 8),)),
        "text_head": centred(splits[3], (D, E), D ** -0.5, 0.1875, ((0, 8),)),
        "logit_scale": jnp.clip(jnp.exp(jax.random.uniform(splits[4], (1,), jnp.float32, math.log(4.0), math.log(12.0))), 4.0, 12.0),
        "logit_bias": jnp.clip(jax.random.uniform(splits[5], (1,), jnp.float32, -4.0, -1.0), -4.0, -1.0),
    }


def unit(raw):
    mean_sq = lax.optimization_barrier(jnp.mean(raw * raw, axis=-1, keepdims=True))
    return raw * lax.rsqrt(mean_sq + 1e-06) / jnp.sqrt(jnp.float32(E))

def back(raw, grad):
    mean_sq = lax.optimization_barrier(jnp.mean(raw * raw, axis=-1, keepdims=True))
    factor = lax.rsqrt(mean_sq + 1e-06) / jnp.sqrt(jnp.float32(E))
    inner = lax.optimization_barrier(jnp.sum(grad * raw, axis=-1, keepdims=True))
    return factor * grad - raw * factor * inner / (E * (mean_sq + 1e-06))

def reference(image_feat, text_feat, image_head, text_head, logit_scale, logit_bias):
    image_raw = jnp.dot(image_feat, image_head, preferred_element_type=jnp.float32)
    text_raw = jnp.dot(text_feat, text_head, preferred_element_type=jnp.float32)
    image_unit = unit(image_raw).astype(jnp.bfloat16)
    text_unit = unit(text_raw).astype(jnp.bfloat16)
    coef = logit_scale[0] / jnp.sqrt(jnp.float32(BATCH))
    columns = jnp.arange(BATCH, dtype=jnp.int32)
    blocks = image_unit.reshape(BATCH // PAIRS_DEV, PAIRS_DEV, E)

    def step(carry, item):
        index, block = item
        rows_idx = index * PAIRS_DEV + jnp.arange(PAIRS_DEV, dtype=jnp.int32)
        scores = logit_scale[0] * jnp.dot(block, text_unit.T, preferred_element_type=jnp.float32) + logit_bias[0]
        match = (rows_idx[:, None] == columns[None, :]).astype(jnp.float32)
        weight = (jax.nn.sigmoid(scores) - match).astype(jnp.bfloat16)
        losses = lax.optimization_barrier(jnp.sum(jax.nn.softplus(scores) - match * scores, axis=1)) / BATCH
        image_part = coef * jnp.dot(weight, text_unit, preferred_element_type=jnp.float32)
        carry = carry + coef * jnp.dot(weight.T, block, preferred_element_type=jnp.float32)
        return (carry, (image_part, losses))
    text_grad, (image_grad, row_loss) = lax.scan(step, jnp.zeros((BATCH, E), jnp.float32), (jnp.arange(BATCH // PAIRS_DEV, dtype=jnp.int32), blocks))
    image_grad = image_grad.reshape(BATCH, E)
    row_loss = row_loss.reshape(BATCH)
    image_back = back(image_raw, image_grad).astype(jnp.bfloat16)
    text_back = back(text_raw, text_grad).astype(jnp.bfloat16)
    grad_image_head = jnp.dot(image_feat.T, image_back, preferred_element_type=jnp.float32)
    grad_text_head = jnp.dot(text_feat.T, text_back, preferred_element_type=jnp.float32)
    return (grad_image_head, grad_text_head, row_loss)
```

```python
import math

import jax
import jax.numpy as jnp
from jax import lax
from jax.sharding import Mesh, PartitionSpec as P

BF = jnp.bfloat16
F32 = jnp.float32
T = ("yl", "x")
ZY = ("z", "yh")
SWAP = [(0, 1), (1, 0)]


def spread(x, axes, n):
    wide = jnp.broadcast_to(x[None], (n,) + x.shape)
    return lax.all_to_all(wide, axes, 0, 0, tiled=True)


def stats(raw):
    width = raw.shape[-1]
    mean_sq = jnp.mean(raw * raw, axis=-1, keepdims=True)
    factor = lax.rsqrt(mean_sq + 1e-06) / math.sqrt(width)
    return factor, 1.0 / (width * (mean_sq + 1e-06))


def back(raw, grad, factor, inv):
    inner = jnp.sum(grad * raw, axis=-1, keepdims=True)
    return factor * (grad - raw * (inner * inv))


def rows_dot(left, right):
    return lax.dot_general(
        left, right, (((0,), (0,)), ((), ())), preferred_element_type=F32
    )


def on_device(image_feat, text_feat, image_head, text_head, logit_scale, logit_bias):
    nz, nt = lax.axis_size("z"), lax.axis_size("yl") * lax.axis_size("x")
    ny = lax.axis_size("yh")
    pairs, depth = image_feat.shape
    width = image_head.shape[1]
    half = depth // 2
    rows = pairs // nt
    core = lax.axis_index("core")
    z = lax.axis_index("z")
    yh = lax.axis_index("yh")
    t = lax.axis_index(T)
    batch = pairs * nz * ny * 2
    coef = logit_scale[0] * (1.0 / math.sqrt(batch))

    def turn(x, axis):
        a = lax.slice_in_dim(x, 0, half, axis=axis)
        b = lax.slice_in_dim(x, half, 2 * half, axis=axis)
        first = core == 0
        return jnp.where(first, a, b), jnp.where(first, b, a)

    text = jnp.concatenate(turn(text_feat, 1), axis=1)
    text = lax.all_to_all(text.reshape(nt, rows, depth), T, 0, 0, tiled=True)
    text = text.reshape(nt, rows, 2, half).transpose(1, 2, 0, 3).reshape(rows, nt * depth)
    text_yh = lax.ppermute(text, "yh", SWAP)
    low = yh == 0
    block = jnp.stack([jnp.where(low, text, text_yh), jnp.where(low, text_yh, text)])

    image = jnp.stack(turn(image_feat.T, 0))
    image = spread(image, T, nt).reshape(nt, 2, half, pairs)
    image = image.transpose(1, 0, 2, 3).reshape(nt * depth, pairs)
    image_other = lax.ppermute(image, "core", SWAP)
    image_other = jnp.concatenate(
        [image_other[nt * half:], image_other[: nt * half]], axis=0
    )
    image = jnp.concatenate([image, image_other], axis=1)

    heads = jnp.stack([turn(image_head, 0)[0], turn(text_head, 0)[0]])
    heads = spread(heads, T, nt).transpose(1, 0, 2, 3).reshape(2, nt * half, width)
    heads_other = lax.ppermute(heads, "core", SWAP)
    head_i = jnp.concatenate([heads[0], heads_other[0]], axis=0)
    head_t = jnp.concatenate([heads[1], heads_other[1]], axis=0)

    up = [(i, (i + 1) % nz) for i in range(nz)]
    down = [(i, (i - 1) % nz) for i in range(nz)]
    blocks = {0: block}
    fwd = bwd = block
    for k in range(1, nz // 2):
        fwd = lax.ppermute(fwd, "z", up)
        bwd = lax.ppermute(bwd, "z", down)
        blocks[-k] = fwd
        blocks[k] = bwd
    blocks[nz // 2] = jnp.stack(
        [lax.ppermute(fwd[0], "z", up), lax.ppermute(bwd[1], "z", down)]
    )
    order = [0]
    for k in range(1, nz // 2):
        order += [-k, k]
    order += [nz // 2]
    texts = jnp.stack([blocks[k] for k in order]).reshape(nz * ny * rows, nt * depth)

    raw_i = rows_dot(image, head_i)
    raw_t = jnp.dot(texts, head_t, preferred_element_type=F32)
    fac_i, inv_i = stats(raw_i)
    fac_t, inv_t = stats(raw_t)
    unit_i = (raw_i * fac_i).astype(BF)
    unit_t = (raw_t * fac_t).astype(BF)

    group = (z * ny + yh) * 2
    r = jnp.arange(pairs, dtype=jnp.int32)
    image_id = jnp.concatenate([(group + core) * pairs + r, (group + 1 - core) * pairs + r])
    src = jnp.concatenate(
        [lax.rem(z + jnp.full((ny * rows,), k + nz, jnp.int32), nz) for k in order]
    )
    local = jnp.arange(nz * ny * rows, dtype=jnp.int32)
    text_id = ((src * ny + local // rows % ny) * 2 + core) * pairs + t * rows + local % rows

    dots = lax.dot_general(
        unit_i, unit_t, (((1,), (1,)), ((), ())), preferred_element_type=F32
    )
    scores = logit_scale[0] * dots + logit_bias[0]
    match = image_id[:, None] == text_id[None, :]
    weight = (jax.nn.sigmoid(scores) - match.astype(F32)).astype(BF)
    losses = jnp.sum(jax.nn.softplus(scores) - jnp.where(match, scores, 0.0), axis=1)

    grad_i = coef * jnp.dot(weight, unit_t, preferred_element_type=F32)
    back_i = back(raw_i, grad_i, fac_i, inv_i).astype(BF)
    part_i = jnp.dot(image, back_i, preferred_element_type=F32)
    grad_t = coef * rows_dot(weight, unit_i)
    back_t = back(raw_t, grad_t, fac_t, inv_t).astype(BF)
    part_t = rows_dot(texts, back_t)

    loss = losses[:pairs] + lax.ppermute(losses[pairs:], "core", SWAP)
    row_loss = jnp.sum(spread(loss, T, nt).reshape(nt, pairs), axis=0) / batch

    def over_t(part):
        other = lax.ppermute(part[nt * half:].astype(BF), "core", SWAP)
        mine = (part[: nt * half] + other.astype(F32)).astype(BF)
        mine = lax.all_to_all(mine.reshape(nt, half, width), T, 0, 0, tiled=True)
        return jnp.sum(mine.astype(F32), axis=0)

    both = jnp.concatenate([over_t(part_i), over_t(part_t)], axis=0)
    n = nz * ny
    both = both.astype(BF).reshape(n, 2 * half // n, width)
    both = lax.all_to_all(both, ZY, 0, 0, tiled=True)
    both = jnp.sum(both.astype(F32), axis=0).astype(BF)
    both = spread(both, ZY, n).reshape(2, half, width)
    other = lax.ppermute(both, "core", SWAP)
    first = core == 0
    low = jnp.where(first, both, other)
    high = jnp.where(first, other, both)
    out = jnp.concatenate([low, high], axis=1).astype(F32)
    return out[0], out[1], row_loss


def solution(mesh):
    fine = Mesh(mesh.devices.reshape(8, 2, 2, 2, 4), ("z", "yh", "core", "yl", "x"))
    dp = ("z", "yh", "core")
    placed = (P(dp, T), P(dp, T), P(T, None), P(T, None), P(), P())
    return jax.shard_map(
        on_device,
        mesh=fine,
        in_specs=placed,
        out_specs=(P(T, None), P(T, None), P(dp)),
        check_vma=False,
    )
```

```python
import functools
import math

import jax
import jax.numpy as jnp
from jax import lax
from jax.experimental import pallas as pl
from jax.experimental.pallas import tpu as pltpu
from jax.sharding import Mesh, PartitionSpec as P

BF = jnp.bfloat16
F32 = jnp.float32
T = ("yl", "x")
PLANE = ("yh", "yl", "x")
SWAP = [(0, 1), (1, 0)]
LANE = 128
TILE = 256
LIMIT = 58 * 1024 * 1024


def spread(x, axes, n):
    wide = jnp.broadcast_to(x[None], (n,) + x.shape)
    return lax.all_to_all(wide, axes, 0, 0, tiled=True)


def contract(left, right, dims):
    return lax.dot_general(left, right, ((dims[:1], dims[1:]), ((), ())), preferred_element_type=F32)


def stats(raw):
    width = raw.shape[-1]
    mean_sq = jnp.mean(raw * raw, axis=-1, keepdims=True)
    return lax.rsqrt(mean_sq + 1e-06) * (1.0 / math.sqrt(width)), 1.0 / (width * (mean_sq + 1e-06))


def back(raw, grad):
    factor, inv = stats(raw)
    inner = jnp.sum(grad * raw, axis=-1, keepdims=True)
    return (factor * (grad - raw * (inner * inv))).astype(BF)


def head_copies(src, dst, sems, first):
    nt, nb = dst.shape[0], dst.shape[2] // LANE
    low = src.shape[1] if first is None else first
    out = []
    for b in range(nb):
        y, s = (0, b) if b < low else (1, b - nb + low)
        out.append(
            pltpu.make_async_copy(
                src.at[pl.ds(y * nt, nt), s], dst.at[:, :, pl.ds(b * LANE, LANE)], sems.at[b]
            )
        )
    return out


def split_rows(part, core, keep, give, head, t):
    half = part.shape[0] // 2
    low, high = part[:half], part[half:]
    first = core == 0
    keep[t, head] = jnp.where(first, low, high)
    give[t, head] = jnp.where(first, high, low).astype(BF)


def block_kernel(
    low, info, scalars, ids, packed, other, text_a, text_b,
    keep, give, loss,
    head_i, head_t, image, texts, raw_t, unit_t, unit_i, weight, backs, part, sems,
):
    nt, depth, width = head_i.shape
    full = nt * depth
    ni, nj = image.shape[2], texts.shape[0]
    core = info[0]
    scale, bias, coef = scalars[0], scalars[1], scalars[2]

    nb = width // LANE
    text_copies = [
        pltpu.make_async_copy(text_a, texts.at[pl.ds(0, nj // 2)], sems.at[2 * nb]),
        pltpu.make_async_copy(text_b, texts.at[pl.ds(nj // 2, nj // 2)], sems.at[2 * nb + 1]),
    ]
    half = ni // LANE // 2
    image_copies = [
        pltpu.make_async_copy(
            packed.at[pl.ds((b // half) * nt, nt), low + b % half],
            image.at[:, :, pl.ds(b * LANE, LANE)],
            sems.at[2 * nb + 2 + b],
        )
        for b in range(2 * half)
    ]
    sems_i, sems_t = sems.at[pl.ds(0, nb)], sems.at[pl.ds(nb, nb)]
    for copy in text_copies:
        copy.start()

    @pl.when(core == 0)
    def _():
        for copy in head_copies(other, head_t, sems_t, low):
            copy.start()
        for copy in head_copies(packed, head_i, sems_i, low):
            copy.start()

    @pl.when(core != 0)
    def _():
        for copy in head_copies(packed, head_t, sems_t, low):
            copy.start()
        for copy in head_copies(other, head_i, sems_i, low):
            copy.start()

    for copy in image_copies:
        copy.start()
    for copy in text_copies + head_copies(packed, head_t, sems_t, low):
        copy.wait()

    @pl.loop(0, nj // TILE)
    def _(j):
        here = pl.ds(pl.multiple_of(j * TILE, TILE), TILE)
        raw = contract(texts[here], head_t[...].reshape(full, width), (1, 0))
        raw_t[here] = raw
        unit_t[here] = (raw * stats(raw)[0]).astype(BF)

    for copy in head_copies(packed, head_i, sems_i, low) + image_copies:
        copy.wait()

    @pl.loop(0, ni // TILE)
    def _(i):
        here = pl.ds(pl.multiple_of(i * TILE, TILE), TILE)
        tile = image[:, :, here].reshape(full, TILE)
        raw = contract(tile, head_i[...].reshape(full, width), (0, 0))
        unit = (raw * stats(raw)[0]).astype(BF)
        unit_i[here] = unit
        scores = scale * contract(unit, unit_t[...], (1, 1)) + bias
        per = ni // 2 // TILE
        base = jnp.where(i < per, info[1], info[2]) + lax.rem(i, per) * TILE
        rows = base + lax.broadcasted_iota(jnp.int32, (TILE, 1), 0)
        match = rows == ids[...]
        small = jnp.exp(-jnp.abs(scores))
        soft = jnp.maximum(scores, 0.0) + jnp.log1p(small)
        sig = jnp.where(scores >= 0.0, 1.0, small) / (1.0 + small)
        terms = soft - jnp.where(match, scores, 0.0)
        total = terms[:, :LANE]
        for b in range(1, nj // LANE):
            total = total + terms[:, b * LANE : (b + 1) * LANE]
        loss[here] = total
        grads = jnp.where(match, sig - 1.0, sig).astype(BF)
        weight[here] = grads
        grad = coef * contract(grads, unit_t[...], (1, 0))
        backs[here] = back(raw, grad)

    @pl.loop(0, nt // 2)
    def _(k):
        rows = contract(image[pl.ds(2 * k, 2)].reshape(2 * depth, ni), backs[...], (1, 0))
        split_rows(rows[:depth], core, keep, give, 0, 2 * k)
        split_rows(rows[depth:], core, keep, give, 0, 2 * k + 1)

    for j in range(nj // TILE):
        here = pl.ds(j * TILE, TILE)
        grad = coef * contract(weight[:, here], unit_i[...], (0, 0))
        backs[here] = back(raw_t[here], grad)

    step = 3 * LANE
    for k in range(full // step):
        here = pl.ds(k * step, step)
        part[here] = contract(texts[:, here], backs[...], (0, 0))

    @pl.loop(0, nt)
    def _(k):
        rows = part[pl.ds(pl.multiple_of(k * depth, depth), depth)]
        split_rows(rows, core, keep, give, 1, k)


def on_device(image_feat, text_feat, image_head, text_head, logit_scale, logit_bias):
    nz, ny = lax.axis_size("z"), lax.axis_size("yh")
    nt = lax.axis_size("yl") * lax.axis_size("x")
    pairs, depth = image_feat.shape
    width = image_head.shape[1]
    half = depth // 2
    rows = pairs // nt
    full = nt * depth
    core = lax.axis_index("core")
    z = lax.axis_index("z")
    yh = lax.axis_index("yh")
    t = lax.axis_index(T)
    batch = pairs * nz * ny * 2
    coef = logit_scale[0] * (1.0 / math.sqrt(batch))

    nb = width // LANE
    low = -(-nb // 2)
    head = jnp.where(core == 0, image_head, text_head).reshape(depth, nb, LANE)
    head = jnp.where(yh == 0, head[:, :low], head[:, nb - low :]).transpose(1, 0, 2)
    columns = image_feat.T.reshape(depth, pairs // LANE, LANE).transpose(1, 0, 2)
    packed = lax.all_gather(jnp.concatenate([head, columns], axis=0), PLANE, axis=0)

    split = text_feat.reshape(nt, rows, depth)
    own = lax.all_to_all(split, T, 0, 0, tiled=True).transpose(1, 0, 2).reshape(rows, full)
    text_a = spread(own, "z", nz).reshape(nz * rows, full)
    text_b = lax.ppermute(text_a, "core", SWAP)
    packed, text_a, text_b = lax.optimization_barrier((packed, text_a, text_b))
    other = lax.ppermute(packed[:, :low], "core", SWAP)

    k = jnp.arange(nz * rows, dtype=jnp.int32)
    ids = jnp.concatenate(
        [((k // rows * ny + yh) * 2 + c) * pairs + t * rows + k % rows for c in (core, 1 - core)]
    )[None]
    info = jnp.stack([core] + [((z * ny + y) * 2 + core) * pairs for y in range(ny)])
    scalars = jnp.stack([logit_scale[0], logit_bias[0], coef])

    ni, nj = ny * pairs, 2 * nz * rows
    smem = pl.BlockSpec(memory_space=pltpu.SMEM)
    vmem = pl.BlockSpec(memory_space=pltpu.VMEM)
    hbm = pl.BlockSpec(memory_space=pl.ANY)
    keep, give, losses = pl.pallas_call(
        functools.partial(block_kernel, low),
        out_shape=[
            jax.ShapeDtypeStruct((nt, 2, half, width), F32),
            jax.ShapeDtypeStruct((nt, 2, half, width), BF),
            jax.ShapeDtypeStruct((ni, LANE), F32),
        ],
        in_specs=[smem, smem, vmem, hbm, hbm, hbm, hbm],
        out_specs=[vmem, vmem, vmem],
        scratch_shapes=[
            pltpu.VMEM((nt, depth, width), BF),
            pltpu.VMEM((nt, depth, width), BF),
            pltpu.VMEM((nt, depth, ni), BF),
            pltpu.VMEM((nj, full), BF),
            pltpu.VMEM((nj, width), F32),
            pltpu.VMEM((nj, width), BF),
            pltpu.VMEM((ni, width), BF),
            pltpu.VMEM((ni, nj), BF),
            pltpu.VMEM((max(ni, nj), width), BF),
            pltpu.VMEM((full, width), F32),
            pltpu.SemaphoreType.DMA((2 * nb + 2 + ni // LANE,)),
        ],
        compiler_params=pltpu.CompilerParams(vmem_limit_bytes=LIMIT),
        cost_estimate=pl.CostEstimate(
            flops=4 * (ni + nj) * full * width + 6 * ni * nj * width,
            bytes_accessed=20 * 1024 * 1024,
            transcendentals=3 * ni * nj,
        ),
        name="block",
    )(info, scalars, ids, packed, other, text_a, text_b)

    low_y = yh == 0
    losses = jnp.sum(losses, axis=1).reshape(ny, pairs)
    loss_mine = jnp.where(low_y, losses[0], losses[1])
    loss_give = jnp.where(low_y, losses[1], losses[0])
    loss = loss_mine + lax.ppermute(loss_give, "yh", SWAP)
    head_part = lax.reduce_precision(loss, 8, 7)
    row = jnp.concatenate([head_part, loss - head_part]).astype(BF)
    row = jnp.pad(row[None], ((0, 7), (0, width - 2 * pairs)))
    mine = (keep + lax.ppermute(give, "core", SWAP).astype(F32)).astype(BF)
    mine = mine.reshape(nt, 2 * half, width)
    mine = jnp.concatenate([mine, jnp.broadcast_to(row[None], (nt,) + row.shape)], axis=1)
    mine = lax.all_to_all(mine, T, 0, 0, tiled=True).astype(F32)
    row = jnp.sum(mine[:, 2 * half], axis=0)
    row_loss = (row[:pairs] + row[pairs : 2 * pairs]) / batch
    both = jnp.sum(mine[:, : 2 * half], axis=0).reshape(2, half, width)
    keep = jnp.where(low_y, both[0], both[1])
    give = jnp.where(low_y, both[1], both[0]).astype(BF)
    one = keep + lax.ppermute(give, "yh", SWAP).astype(F32)

    tiles = (half // 8) * nb
    per = -(-tiles // nz)
    one = one.astype(BF).reshape(half // 8, 8, nb, LANE).transpose(0, 2, 1, 3)
    one = jnp.pad(one.reshape(tiles, 8, LANE), ((0, per * nz - tiles), (0, 0), (0, 0)))
    one = lax.all_to_all(one.reshape(nz, per * 8, LANE), "z", 0, 0, tiled=True)
    one = jnp.sum(one.astype(F32), axis=0).astype(BF)
    one = spread(one, "z", nz).reshape(per * nz, 8, LANE)[:tiles]
    one = one.reshape(half // 8, nb, 8, LANE).transpose(0, 2, 1, 3).reshape(half, width)
    by_core = lax.ppermute(one, "core", SWAP)
    by_y = lax.ppermute(one, "yh", SWAP)
    by_both = lax.ppermute(one, ("yh", "core"), [(0, 3), (1, 2), (2, 1), (3, 0)])

    def join(mine, other):
        first = core == 0
        return jnp.concatenate([jnp.where(first, mine, other), jnp.where(first, other, mine)])

    here, there = join(one, by_core), join(by_y, by_both)
    out_i = jnp.where(low_y, here, there).astype(F32)
    out_t = jnp.where(low_y, there, here).astype(F32)
    return out_i, out_t, row_loss


def solution(mesh):
    fine = Mesh(mesh.devices.reshape(8, 2, 2, 2, 4), ("z", "yh", "core", "yl", "x"))
    dp = ("z", "yh", "core")
    placed = (P(dp, T), P(dp, T), P(T, None), P(T, None), P(), P())
    return jax.shard_map(
        on_device,
        mesh=fine,
        in_specs=placed,
        out_specs=(P(T, None), P(T, None), P(dp)),
        check_vma=False,
    )
```

```python
import functools
import math

import jax
import jax.numpy as jnp
from jax import lax
from jax.experimental import pallas as pl
from jax.experimental.pallas import tpu as pltpu
from jax.sharding import Mesh, PartitionSpec as P

BF = jnp.bfloat16
F32 = jnp.float32
T = ("yl", "x")
PLANE = ("yh", "yl", "x")
ZY = ("z", "yh")
SWAP = [(0, 1), (1, 0)]
LANE = 128
TILE = 512
LIMIT = 58 * 1024 * 1024


def spread(x, axes, n):
    wide = jnp.broadcast_to(x[None], (n,) + x.shape)
    return lax.all_to_all(wide, axes, 0, 0, tiled=True)


def contract(left, right, dims):
    return lax.dot_general(left, right, ((dims[:1], dims[1:]), ((), ())), preferred_element_type=F32)


def stats(raw):
    width = raw.shape[-1]
    mean_sq = jnp.mean(raw * raw, axis=-1, keepdims=True)
    return lax.rsqrt(mean_sq + 1e-06) * (1.0 / math.sqrt(width)), 1.0 / (width * (mean_sq + 1e-06))


def back(raw, grad):
    factor, inv = stats(raw)
    inner = jnp.sum(grad * raw, axis=-1, keepdims=True)
    return (factor * (grad - raw * (inner * inv))).astype(BF)


def head_copies(src, dst, sems, first):
    nt, nb = dst.shape[0], dst.shape[2] // LANE
    low = src.shape[1] if first is None else first
    out = []
    for b in range(nb):
        y, s = (0, b) if b < low else (1, b - nb + low)
        out.append(
            pltpu.make_async_copy(
                src.at[pl.ds(y * nt, nt), s], dst.at[:, :, pl.ds(b * LANE, LANE)], sems.at[b]
            )
        )
    return out


def block_kernel(
    low, info, scalars, ids, packed, other, text_a, text_b,
    keep, give, loss,
    head_i, head_t, image, texts, raw_t, unit_t, unit_i, weight, backs, part_i, part_t, sems, out_sems,
):
    nt, depth, width = head_i.shape
    full = nt * depth
    ni, nj = image.shape[2], texts.shape[0]
    core = info[0]
    scale, bias, coef = scalars[0], scalars[1], scalars[2]

    nb = width // LANE
    text_copies = [
        pltpu.make_async_copy(text_a, texts.at[pl.ds(0, nj // 2)], sems.at[2 * nb]),
        pltpu.make_async_copy(text_b, texts.at[pl.ds(nj // 2, nj // 2)], sems.at[2 * nb + 1]),
    ]
    half = ni // LANE // 2
    image_copies = [
        pltpu.make_async_copy(
            packed.at[pl.ds((b // half) * nt, nt), low + b % half],
            image.at[:, :, pl.ds(b * LANE, LANE)],
            sems.at[2 * nb + 2 + b],
        )
        for b in range(2 * half)
    ]
    sems_i, sems_t = sems.at[pl.ds(0, nb)], sems.at[pl.ds(nb, nb)]

    def start_head(dst, at, mine):
        @pl.when(core == mine)
        def _():
            for copy in head_copies(packed, dst, at, low):
                copy.start()

        @pl.when(core != mine)
        def _():
            for copy in head_copies(other, dst, at, low):
                copy.start()

    for copy in text_copies:
        copy.start()
    start_head(head_t, sems_t, 1)
    for copy in text_copies + head_copies(packed, head_t, sems_t, low):
        copy.wait()
    start_head(head_i, sems_i, 0)
    for copy in image_copies:
        copy.start()

    @pl.loop(0, nj // TILE)
    def _(j):
        here = pl.ds(pl.multiple_of(j * TILE, TILE), TILE)
        raw = contract(texts[here], head_t[...].reshape(full, width), (1, 0))
        raw_t[here] = raw
        unit_t[here] = (raw * stats(raw)[0]).astype(BF)

    for copy in head_copies(packed, head_i, sems_i, low) + image_copies:
        copy.wait()

    for i in range(ni // TILE):
        here = pl.ds(i * TILE, TILE)
        tile = image[:, :, here].reshape(full, TILE)
        raw = contract(tile, head_i[...].reshape(full, width), (0, 0))
        unit = (raw * stats(raw)[0]).astype(BF)
        unit_i[here] = unit
        scores = scale * contract(unit, unit_t[...], (1, 1)) + bias
        per = ni // 2 // TILE
        base = info[1 + i // per] + i % per * TILE
        rows = base + lax.broadcasted_iota(jnp.int32, (TILE, 1), 0)
        match = rows == ids[...]
        small = jnp.exp(-jnp.abs(scores))
        soft = jnp.maximum(scores, 0.0) + jnp.log1p(small)
        sig = jnp.where(scores >= 0.0, 1.0, small) / (1.0 + small)
        terms = soft - jnp.where(match, scores, 0.0)
        total = terms[:, :LANE]
        for b in range(1, nj // LANE):
            total = total + terms[:, b * LANE : (b + 1) * LANE]
        loss[:, here] = jnp.sum(total.T, axis=0, keepdims=True)
        grads = jnp.where(match, sig - 1.0, sig).astype(BF)
        weight[here] = grads
        grad = coef * contract(grads, unit_t[...], (1, 0))
        backs[here] = back(raw, grad)

    step = 3 * LANE

    def out_copy(src, dst, at, k):
        here = pl.ds(k * step, step)
        return pltpu.make_async_copy(src.at[here], dst.at[here], out_sems.at[at + k])

    def send(src, at, mine, k):
        @pl.when(core == mine)
        def _():
            out_copy(src, keep, at, k).start()

        @pl.when(core != mine)
        def _():
            out_copy(src, give, at, k).start()

    wide = nt // 2 * depth
    for k in range(2):
        rows = image[pl.ds(k * nt // 2, nt // 2)].reshape(wide, ni)
        part_i[pl.ds(k * wide, wide)] = contract(rows, backs[...], (1, 0)).astype(BF)
    for k in range(full // step):
        send(part_i, 0, 0, k)

    for j in range(nj // TILE):
        here = pl.ds(j * TILE, TILE)
        grad = coef * contract(weight[:, here], unit_i[...], (0, 0))
        backs[here] = back(raw_t[here], grad)

    for k in range(full // step):
        here = pl.ds(k * step, step)
        part_t[here] = contract(texts[:, here], backs[...], (0, 0)).astype(BF)
        send(part_t, full // step, 1, k)

    for k in range(full // step):
        out_copy(part_i, keep, 0, k).wait()
        out_copy(part_t, give, full // step, k).wait()


def on_device(image_feat, text_feat, image_head, text_head, logit_scale, logit_bias):
    nz, ny = lax.axis_size("z"), lax.axis_size("yh")
    nt = lax.axis_size("yl") * lax.axis_size("x")
    pairs, depth = image_feat.shape
    width = image_head.shape[1]
    rows = pairs // nt
    full = nt * depth
    core = lax.axis_index("core")
    z = lax.axis_index("z")
    yh = lax.axis_index("yh")
    t = lax.axis_index(T)
    batch = pairs * nz * ny * 2
    coef = logit_scale[0] * (1.0 / math.sqrt(batch))

    nb = width // LANE
    low = -(-nb // 2)
    head = jnp.where(core == 0, image_head, text_head).reshape(depth, nb, LANE)
    head = jnp.where(yh == 0, head[:, :low], head[:, nb - low :]).transpose(1, 0, 2)
    columns = image_feat.T.reshape(depth, pairs // LANE, LANE).transpose(1, 0, 2)
    packed = lax.all_gather(jnp.concatenate([head, columns], axis=0), PLANE, axis=0)

    split = text_feat.reshape(nt, rows, depth)
    own = lax.all_to_all(split, T, 0, 0, tiled=True).transpose(1, 0, 2).reshape(rows, full)
    text_a = spread(own, "z", nz).reshape(nz * rows, full)
    text_b = lax.ppermute(text_a, "core", SWAP)
    k = jnp.arange(nz * rows, dtype=jnp.int32)
    ids = jnp.concatenate(
        [((k // rows * ny + yh) * 2 + c) * pairs + t * rows + k % rows for c in (core, 1 - core)]
    )[None]
    info = jnp.stack([core] + [((z * ny + y) * 2 + core) * pairs for y in range(ny)])
    scalars = jnp.stack([logit_scale[0], logit_bias[0], coef])

    packed, text_a, text_b, ids, info, scalars = lax.optimization_barrier(
        (packed, text_a, text_b, ids, info, scalars)
    )
    other = lax.ppermute(packed[:, :low], "core", SWAP)

    ni, nj = ny * pairs, 2 * nz * rows
    smem = pl.BlockSpec(memory_space=pltpu.SMEM)
    vmem = pl.BlockSpec(memory_space=pltpu.VMEM)
    hbm = pl.BlockSpec(memory_space=pl.ANY)
    keep, give, losses = pl.pallas_call(
        functools.partial(block_kernel, low),
        out_shape=[
            jax.ShapeDtypeStruct((full, width), BF),
            jax.ShapeDtypeStruct((full, width), BF),
            jax.ShapeDtypeStruct((1, ni), F32),
        ],
        in_specs=[smem, smem, vmem, hbm, hbm, hbm, hbm],
        out_specs=[hbm, hbm, vmem],
        scratch_shapes=[
            pltpu.VMEM((nt, depth, width), BF),
            pltpu.VMEM((nt, depth, width), BF),
            pltpu.VMEM((nt, depth, ni), BF),
            pltpu.VMEM((nj, full), BF),
            pltpu.VMEM((nj, width), F32),
            pltpu.VMEM((nj, width), BF),
            pltpu.VMEM((ni, width), BF),
            pltpu.VMEM((ni, nj), BF),
            pltpu.VMEM((max(ni, nj), width), BF),
            pltpu.VMEM((full, width), BF),
            pltpu.VMEM((full, width), BF),
            pltpu.SemaphoreType.DMA((2 * nb + 2 + ni // LANE,)),
            pltpu.SemaphoreType.DMA((2 * (full // (3 * LANE)),)),
        ],
        compiler_params=pltpu.CompilerParams(vmem_limit_bytes=LIMIT),
        cost_estimate=pl.CostEstimate(
            flops=4 * (ni + nj) * full * width + 6 * ni * nj * width,
            bytes_accessed=20 * 1024 * 1024,
            transcendentals=3 * ni * nj,
        ),
        name="block",
    )(info, scalars, ids, packed, other, text_a, text_b)

    low_y = yh == 0
    losses = losses.reshape(ny, pairs)
    loss_mine = jnp.where(low_y, losses[0], losses[1])
    loss_give = jnp.where(low_y, losses[1], losses[0])
    loss = loss_mine + lax.ppermute(loss_give, "yh", SWAP)
    head_part = lax.reduce_precision(loss, 8, 7)
    row = jnp.concatenate([head_part, loss - head_part]).astype(BF)
    row = jnp.pad(row[None], ((0, 7), (0, width - 2 * pairs)))
    mine = (keep.astype(F32) + lax.ppermute(give, "core", SWAP).astype(F32)).astype(BF)
    mine = mine.reshape(nt, depth, width)
    mine = jnp.concatenate([mine, jnp.broadcast_to(row[None], (nt,) + row.shape)], axis=1)
    mine = lax.all_to_all(mine, T, 0, 0, tiled=True).astype(F32)
    row = jnp.sum(mine[:, depth], axis=0)
    row_loss = (row[:pairs] + row[pairs : 2 * pairs]) / batch
    one = jnp.sum(mine[:, :depth], axis=0).astype(BF)

    n = nz * ny
    tiles = (depth // 8) * nb
    per = -(-tiles // n)
    one = one.reshape(depth // 8, 8, nb, LANE).transpose(0, 2, 1, 3)
    one = jnp.pad(one.reshape(tiles, 8, LANE), ((0, per * n - tiles), (0, 0), (0, 0)))
    one = lax.all_to_all(one.reshape(n, per * 8, LANE), ZY, 0, 0, tiled=True)
    one = jnp.sum(one.astype(F32), axis=0).astype(BF)
    one = spread(one, ZY, n).reshape(per * n, 8, LANE)[:tiles]
    one = one.reshape(depth // 8, nb, 8, LANE).transpose(0, 2, 1, 3).reshape(depth, width)
    two = lax.ppermute(one, "core", SWAP)
    out_i = jnp.where(core == 0, one, two).astype(F32)
    out_t = jnp.where(core == 0, two, one).astype(F32)
    return out_i, out_t, row_loss


def solution(mesh):
    fine = Mesh(mesh.devices.reshape(8, 2, 2, 2, 4), ("z", "yh", "core", "yl", "x"))
    dp = ("z", "yh", "core")
    placed = (P(dp, T), P(dp, T), P(T, None), P(T, None), P(), P())
    return jax.shard_map(
        on_device,
        mesh=fine,
        in_specs=placed,
        out_specs=(P(T, None), P(T, None), P(dp)),
        check_vma=False,
    )
```

```python
import functools
import math

import jax
import jax.numpy as jnp
from jax import lax
from jax.experimental import pallas as pl
from jax.experimental.pallas import tpu as pltpu
from jax.sharding import Mesh, PartitionSpec as P

BF = jnp.bfloat16
F32 = jnp.float32
T = ("yl", "x")
PLANE = ("yh", "yl", "x")
ZY = ("z", "yh")
SWAP = [(0, 1), (1, 0)]
LANE = 128
TILE = 512
LIMIT = 58 * 1024 * 1024


def spread(x, axes, n):
    wide = jnp.broadcast_to(x[None], (n,) + x.shape)
    return lax.all_to_all(wide, axes, 0, 0, tiled=True)


def contract(left, right, dims):
    return lax.dot_general(left, right, ((dims[:1], dims[1:]), ((), ())), preferred_element_type=F32)


def stats(raw):
    width = raw.shape[-1]
    mean_sq = jnp.mean(raw * raw, axis=-1, keepdims=True)
    return lax.rsqrt(mean_sq + 1e-06) * (1.0 / math.sqrt(width)), 1.0 / (width * (mean_sq + 1e-06))


def back(raw, grad):
    factor, inv = stats(raw)
    inner = jnp.sum(grad * raw, axis=-1, keepdims=True)
    return (factor * (grad - raw * (inner * inv))).astype(BF)


def head_copies(src, dst, sems, first):
    nt, nb = dst.shape[0], dst.shape[2] // LANE
    low = src.shape[1] if first is None else first
    out = []
    for b in range(nb):
        y, s = (0, b) if b < low else (1, b - nb + low)
        out.append(
            pltpu.make_async_copy(
                src.at[pl.ds(y * nt, nt), s], dst.at[:, :, pl.ds(b * LANE, LANE)], sems.at[b]
            )
        )
    return out


def block_kernel(
    low, info, scalars, ids, packed, other, text_a, text_b,
    keep_a, keep_b, give_a, give_b, loss,
    head_i, head_t, image, texts, raw_t, unit_t, unit_i, weight, backs, part_i, part_t, sems, out_sems,
):
    nt, depth, width = head_i.shape
    full = nt * depth
    ni, nj = image.shape[2], texts.shape[0]
    core = info[0]
    scale, bias, coef = scalars[0], scalars[1], scalars[2]

    nb = width // LANE
    text_copies = [
        pltpu.make_async_copy(text_a, texts.at[pl.ds(0, nj // 2)], sems.at[2 * nb]),
        pltpu.make_async_copy(text_b, texts.at[pl.ds(nj // 2, nj // 2)], sems.at[2 * nb + 1]),
    ]
    half = ni // LANE // 2
    image_copies = [
        pltpu.make_async_copy(
            packed.at[pl.ds((b // half) * nt, nt), low + b % half],
            image.at[:, :, pl.ds(b * LANE, LANE)],
            sems.at[2 * nb + 2 + b],
        )
        for b in range(2 * half)
    ]
    sems_i, sems_t = sems.at[pl.ds(0, nb)], sems.at[pl.ds(nb, nb)]

    def start_head(dst, at, mine):
        @pl.when(core == mine)
        def _():
            for copy in head_copies(packed, dst, at, low):
                copy.start()

        @pl.when(core != mine)
        def _():
            for copy in head_copies(other, dst, at, low):
                copy.start()

    for copy in text_copies:
        copy.start()
    start_head(head_t, sems_t, 1)
    for copy in text_copies + head_copies(packed, head_t, sems_t, low):
        copy.wait()
    start_head(head_i, sems_i, 0)
    for copy in image_copies:
        copy.start()

    @pl.loop(0, nj // TILE)
    def _(j):
        here = pl.ds(pl.multiple_of(j * TILE, TILE), TILE)
        raw = contract(texts[here], head_t[...].reshape(full, width), (1, 0))
        raw_t[here] = raw
        unit_t[here] = (raw * stats(raw)[0]).astype(BF)

    for copy in head_copies(packed, head_i, sems_i, low) + image_copies:
        copy.wait()

    for i in range(ni // TILE):
        here = pl.ds(i * TILE, TILE)
        tile = image[:, :, here].reshape(full, TILE)
        raw = contract(tile, head_i[...].reshape(full, width), (0, 0))
        unit = (raw * stats(raw)[0]).astype(BF)
        unit_i[here] = unit
        scores = scale * contract(unit, unit_t[...], (1, 1)) + bias
        per = ni // 2 // TILE
        base = info[1 + i // per] + i % per * TILE
        rows = base + lax.broadcasted_iota(jnp.int32, (TILE, 1), 0)
        match = rows == ids[...]
        small = jnp.exp(-jnp.abs(scores))
        soft = jnp.maximum(scores, 0.0) + jnp.log1p(small)
        sig = jnp.where(scores >= 0.0, 1.0, small) / (1.0 + small)
        terms = soft - jnp.where(match, scores, 0.0)
        total = terms[:, :LANE]
        for b in range(1, nj // LANE):
            total = total + terms[:, b * LANE : (b + 1) * LANE]
        loss[:, here] = jnp.sum(total.T, axis=0, keepdims=True)
        grads = jnp.where(match, sig - 1.0, sig).astype(BF)
        weight[here] = grads
        grad = coef * contract(grads, unit_t[...], (1, 0))
        backs[here] = back(raw, grad)

    step = 3 * LANE

    keep, give = (keep_a, keep_b), (give_a, give_b)
    ny, _, cut = keep_a.shape

    def out_copies(src, dst, at, k):
        here = pl.ds(k * step, step)
        at = at + k * (ny + 1)
        return [
            pltpu.make_async_copy(
                src.at[here, pl.ds(y * cut, cut)], dst[0].at[y, here], out_sems.at[at + y]
            )
            for y in range(ny)
        ] + [
            pltpu.make_async_copy(
                src.at[here, pl.ds(ny * cut, width - ny * cut)], dst[1].at[here], out_sems.at[at + ny]
            )
        ]

    def send(src, at, mine, k):
        @pl.when(core == mine)
        def _():
            for copy in out_copies(src, keep, at, k):
                copy.start()

        @pl.when(core != mine)
        def _():
            for copy in out_copies(src, give, at, k):
                copy.start()

    wide = nt // 2 * depth
    for k in range(2):
        rows = image[pl.ds(k * nt // 2, nt // 2)].reshape(wide, ni)
        part_i[pl.ds(k * wide, wide)] = contract(rows, backs[...], (1, 0)).astype(BF)
    for k in range(full // step):
        send(part_i, 0, 0, k)

    for j in range(nj // TILE):
        here = pl.ds(j * TILE, TILE)
        grad = coef * contract(weight[:, here], unit_i[...], (0, 0))
        backs[here] = back(raw_t[here], grad)

    for k in range(full // step):
        here = pl.ds(k * step, step)
        part_t[here] = contract(texts[:, here], backs[...], (0, 0)).astype(BF)
        send(part_t, full // step * (ny + 1), 1, k)

    for k in range(full // step):
        for copy in out_copies(part_i, keep, 0, k):
            copy.wait()
        for copy in out_copies(part_t, give, full // step * (ny + 1), k):
            copy.wait()


def on_device(image_feat, text_feat, image_head, text_head, logit_scale, logit_bias):
    nz, ny = lax.axis_size("z"), lax.axis_size("yh")
    nt = lax.axis_size("yl") * lax.axis_size("x")
    pairs, depth = image_feat.shape
    width = image_head.shape[1]
    rows = pairs // nt
    full = nt * depth
    core = lax.axis_index("core")
    z = lax.axis_index("z")
    yh = lax.axis_index("yh")
    t = lax.axis_index(T)
    batch = pairs * nz * ny * 2
    coef = logit_scale[0] * (1.0 / math.sqrt(batch))

    nb = width // LANE
    low = -(-nb // 2)
    head = jnp.where(core == 0, image_head, text_head).reshape(depth, nb, LANE)
    head = jnp.where(yh == 0, head[:, :low], head[:, nb - low :]).transpose(1, 0, 2)
    columns = image_feat.T.reshape(depth, pairs // LANE, LANE).transpose(1, 0, 2)
    packed = jnp.concatenate([head, columns], axis=0)
    packed, text_feat = lax.optimization_barrier((packed, text_feat))
    packed = lax.all_gather(packed, PLANE, axis=0)

    split = text_feat.reshape(nt, rows, depth)
    own = lax.all_to_all(split, T, 0, 0, tiled=True).transpose(1, 0, 2).reshape(rows, full)
    text_a = spread(own, "z", nz).reshape(nz * rows, full)
    text_b = lax.ppermute(text_a, "core", SWAP)
    k = jnp.arange(nz * rows, dtype=jnp.int32)
    ids = jnp.concatenate(
        [((k // rows * ny + yh) * 2 + c) * pairs + t * rows + k % rows for c in (core, 1 - core)]
    )[None]
    info = jnp.stack([core] + [((z * ny + y) * 2 + core) * pairs for y in range(ny)])
    scalars = jnp.stack([logit_scale[0], logit_bias[0], coef])

    packed, text_a, text_b, ids, info, scalars = lax.optimization_barrier(
        (packed, text_a, text_b, ids, info, scalars)
    )
    other = lax.ppermute(packed[:, :low], "core", SWAP)

    ni, nj = ny * pairs, 2 * nz * rows
    smem = pl.BlockSpec(memory_space=pltpu.SMEM)
    vmem = pl.BlockSpec(memory_space=pltpu.VMEM)
    hbm = pl.BlockSpec(memory_space=pl.ANY)
    cut = width // LANE // 3 * LANE
    sums = [
        jax.ShapeDtypeStruct((ny, full, cut), BF),
        jax.ShapeDtypeStruct((full, width - ny * cut), BF),
    ]
    keep_a, keep_b, give_a, give_b, losses = pl.pallas_call(
        functools.partial(block_kernel, low),
        out_shape=[
            *sums,
            *sums,
            jax.ShapeDtypeStruct((1, ni), F32),
        ],
        in_specs=[smem, smem, vmem, hbm, hbm, hbm, hbm],
        out_specs=[hbm, hbm, hbm, hbm, vmem],
        scratch_shapes=[
            pltpu.VMEM((nt, depth, width), BF),
            pltpu.VMEM((nt, depth, width), BF),
            pltpu.VMEM((nt, depth, ni), BF),
            pltpu.VMEM((nj, full), BF),
            pltpu.VMEM((nj, width), F32),
            pltpu.VMEM((nj, width), BF),
            pltpu.VMEM((ni, width), BF),
            pltpu.VMEM((ni, nj), BF),
            pltpu.VMEM((max(ni, nj), width), BF),
            pltpu.VMEM((full, width), BF),
            pltpu.VMEM((full, width), BF),
            pltpu.SemaphoreType.DMA((2 * nb + 2 + ni // LANE,)),
            pltpu.SemaphoreType.DMA((2 * (full // (3 * LANE)) * (ny + 1),)),
        ],
        compiler_params=pltpu.CompilerParams(vmem_limit_bytes=LIMIT),
        cost_estimate=pl.CostEstimate(
            flops=4 * (ni + nj) * full * width + 6 * ni * nj * width,
            bytes_accessed=20 * 1024 * 1024,
            transcendentals=3 * ni * nj,
        ),
        name="block",
    )(info, scalars, ids, packed, other, text_a, text_b)

    nx, nyl = lax.axis_size("x"), lax.axis_size("yl")
    n_y = ny * nyl
    x = lax.axis_index("x")
    half = depth // 2

    def two_parts(loss):
        first = lax.reduce_precision(loss, 8, 7)
        parts = jnp.concatenate([first, loss - first], axis=-1).astype(BF)
        spare = 8 * cut - 2 * pairs
        parts = jnp.pad(parts, [(0, 0)] * (parts.ndim - 1) + [(0, spare)])
        return parts.reshape(parts.shape[:-1] + (8, cut))

    def one_part(rows):
        return jnp.sum(rows.reshape(8 * cut)[: 2 * pairs].reshape(2, pairs), axis=0)

    def over_x(chunk):
        total = chunk(x).astype(F32)
        for k in range(1, nx):
            part = chunk(lax.rem(x + k, nx)).astype(BF)
            total = total + lax.ppermute(part, "x", [(i, (i + k) % nx) for i in range(nx)]).astype(F32)
        return total

    def core_sum(mine, other):
        return (mine.astype(F32) + lax.ppermute(other, "core", SWAP).astype(F32)).astype(BF)

    a = core_sum(keep_a, give_a).reshape(ny, nyl, nx * depth, cut)
    row = jnp.broadcast_to(two_parts(losses.reshape(ny, pairs))[:, None], (ny, nyl, 8, cut))
    a = jnp.concatenate([a, row], axis=2).reshape(n_y, nx * depth + 8, cut)
    a = lax.all_to_all(a, ("yh", "yl"), 0, 0, tiled=True)
    b = core_sum(keep_b, give_b).reshape(nyl, nx, depth, width - ny * cut)
    b = over_x(lambda k: lax.dynamic_index_in_dim(b, k, 1, keepdims=False)).astype(BF)

    a, b = lax.optimization_barrier((a, b))
    a = jnp.sum(a.astype(F32), axis=0)
    row = two_parts(one_part(a[nx * depth :])).astype(F32)
    a = a[: nx * depth].reshape(nx, depth, cut)
    a = over_x(
        lambda k: jnp.concatenate([lax.dynamic_index_in_dim(a, k, 0, keepdims=False), row], axis=0)
    )
    row_loss = one_part(a[depth:]) / batch
    a = a[:depth].astype(BF)
    b = b.reshape(nyl, ny, half, width - ny * cut).transpose(1, 0, 2, 3)
    b = lax.all_to_all(b.reshape(n_y, half, width - ny * cut), ("yh", "yl"), 0, 0, tiled=True)
    b = jnp.sum(b.astype(F32), axis=0).astype(BF)

    def to_tiles(v):
        r, c = v.shape
        return v.reshape(r // 8, 8, c // LANE, LANE).transpose(0, 2, 1, 3).reshape(-1, 8, LANE)

    def from_tiles(v, r, c):
        return v.reshape(r // 8, c // LANE, 8, LANE).transpose(0, 2, 1, 3).reshape(r, c)

    tiles_a = depth // 8 * (cut // LANE)
    one = jnp.concatenate([to_tiles(a), to_tiles(b)], axis=0)
    tiles = one.shape[0]
    per = -(-tiles // nz)
    one = jnp.pad(one, ((0, per * nz - tiles), (0, 0), (0, 0)))
    one = lax.all_to_all(one.reshape(nz, per * 8, LANE), "z", 0, 0, tiled=True)
    one = jnp.sum(one.astype(F32), axis=0).astype(BF)
    one = spread(one, ZY, nz * ny).reshape(nz, ny, per * 8, LANE).transpose(1, 0, 2, 3)
    one = one.reshape(ny, per * nz, 8, LANE)
    left = [from_tiles(one[y, :tiles_a], depth, cut) for y in range(ny)]
    right = [from_tiles(one[y, tiles_a:tiles], half, width - ny * cut) for y in range(ny)]
    one = jnp.concatenate([*left, jnp.concatenate(right, axis=0)], axis=1)
    two = lax.ppermute(one, "core", SWAP)
    out_i = jnp.where(core == 0, one, two).astype(F32)
    out_t = jnp.where(core == 0, two, one).astype(F32)
    return out_i, out_t, row_loss


def solution(mesh):
    fine = Mesh(mesh.devices.reshape(8, 2, 2, 2, 4), ("z", "yh", "core", "yl", "x"))
    dp = ("z", "yh", "core")
    placed = (P(dp, T), P(dp, T), P(T, None), P(T, None), P(), P())
    return jax.shard_map(
        on_device,
        mesh=fine,
        in_specs=placed,
        out_specs=(P(T, None), P(T, None), P(dp)),
        check_vma=False,
    )
```

```python
import functools
import math

import jax
import jax.numpy as jnp
from jax import lax
from jax.experimental import pallas as pl
from jax.experimental.pallas import tpu as pltpu
from jax.sharding import Mesh, PartitionSpec as P

BF = jnp.bfloat16
F32 = jnp.float32
T = ("yl", "x")
PLANE = ("yh", "yl", "x")
ZY = ("z", "yh")
SWAP = [(0, 1), (1, 0)]
LANE = 128
TILE = 512
LIMIT = 58 * 1024 * 1024


def spread(x, axes, n):
    wide = jnp.broadcast_to(x[None], (n,) + x.shape)
    return lax.all_to_all(wide, axes, 0, 0, tiled=True)


def contract(left, right, dims):
    return lax.dot_general(left, right, ((dims[:1], dims[1:]), ((), ())), preferred_element_type=F32)


def stats(raw):
    width = raw.shape[-1]
    mean_sq = jnp.mean(raw * raw, axis=-1, keepdims=True)
    return lax.rsqrt(mean_sq + 1e-06) * (1.0 / math.sqrt(width)), 1.0 / (width * (mean_sq + 1e-06))


def back(raw, grad):
    factor, inv = stats(raw)
    inner = jnp.sum(grad * raw, axis=-1, keepdims=True)
    return (factor * (grad - raw * (inner * inv))).astype(BF)


def head_copies(src, dst, sems, first):
    nt, nb = dst.shape[0], dst.shape[2] // LANE
    low = src.shape[1] if first is None else first
    out = []
    for b in range(nb):
        y, s = (0, b) if b < low else (1, b - nb + low)
        out.append(
            pltpu.make_async_copy(
                src.at[pl.ds(y * nt, nt), s], dst.at[:, :, pl.ds(b * LANE, LANE)], sems.at[b]
            )
        )
    return out


def block_kernel(
    low, info, scalars, ids, packed, other, text_a, text_b,
    keep_a, keep_b, give_a, give_b, loss,
    head_i, head_t, image, texts, raw_t, unit_t, unit_i, weight, backs, part_i, part_t, sems, out_sems,
):
    nt, depth, width = head_i.shape
    full = nt * depth
    ni, nj = image.shape[2], texts.shape[0]
    core = info[0]
    scale, bias, coef = scalars[0], scalars[1], scalars[2]

    nb = width // LANE
    text_copies = [
        pltpu.make_async_copy(text_a, texts.at[pl.ds(0, nj // 2)], sems.at[2 * nb]),
        pltpu.make_async_copy(text_b, texts.at[pl.ds(nj // 2, nj // 2)], sems.at[2 * nb + 1]),
    ]
    half = ni // LANE // 2
    image_copies = [
        pltpu.make_async_copy(
            packed.at[pl.ds((b // half) * nt, nt), low + b % half],
            image.at[:, :, pl.ds(b * LANE, LANE)],
            sems.at[2 * nb + 2 + b],
        )
        for b in range(2 * half)
    ]
    sems_i, sems_t = sems.at[pl.ds(0, nb)], sems.at[pl.ds(nb, nb)]

    def start_head(dst, at, mine):
        @pl.when(core == mine)
        def _():
            for copy in head_copies(packed, dst, at, low):
                copy.start()

        @pl.when(core != mine)
        def _():
            for copy in head_copies(other, dst, at, low):
                copy.start()

    text_copies[0].start()
    start_head(head_t, sems_t, 1)
    for copy in text_copies[:1] + head_copies(packed, head_t, sems_t, low):
        copy.wait()
    text_copies[1].start()
    start_head(head_i, sems_i, 0)
    for copy in image_copies:
        copy.start()

    for j in range(nj // TILE):
        if j * TILE == nj // 2:
            text_copies[1].wait()
        here = pl.ds(j * TILE, TILE)
        raw = contract(texts[here], head_t[...].reshape(full, width), (1, 0))
        raw_t[here] = raw
        unit_t[here] = (raw * stats(raw)[0]).astype(BF)

    for copy in head_copies(packed, head_i, sems_i, low) + image_copies:
        copy.wait()

    for i in range(ni // TILE):
        here = pl.ds(i * TILE, TILE)
        tile = image[:, :, here].reshape(full, TILE)
        raw = contract(tile, head_i[...].reshape(full, width), (0, 0))
        unit = (raw * stats(raw)[0]).astype(BF)
        unit_i[here] = unit
        scores = scale * contract(unit, unit_t[...], (1, 1)) + bias
        per = ni // 2 // TILE
        base = info[1 + i // per] + i % per * TILE
        rows = base + lax.broadcasted_iota(jnp.int32, (TILE, 1), 0)
        match = rows == ids[...]
        small = jnp.exp(-jnp.abs(scores))
        soft = jnp.maximum(scores, 0.0) + jnp.log1p(small)
        sig = jnp.where(scores >= 0.0, 1.0, small) / (1.0 + small)
        terms = soft - jnp.where(match, scores, 0.0)
        total = terms[:, :LANE]
        for b in range(1, nj // LANE):
            total = total + terms[:, b * LANE : (b + 1) * LANE]
        loss[:, here] = jnp.sum(total.T, axis=0, keepdims=True)
        grads = jnp.where(match, sig - 1.0, sig).astype(BF)
        weight[here] = grads
        grad = coef * contract(grads, unit_t[...], (1, 0))
        backs[here] = back(raw, grad)

    step = 3 * LANE

    keep, give = (keep_a, keep_b), (give_a, give_b)
    ny, _, cut = keep_a.shape

    def out_copies(src, dst, at, k):
        here = pl.ds(k * step, step)
        at = at + k * (ny + 1)
        return [
            pltpu.make_async_copy(
                src.at[here, pl.ds(y * cut, cut)], dst[0].at[y, here], out_sems.at[at + y]
            )
            for y in range(ny)
        ] + [
            pltpu.make_async_copy(
                src.at[here, pl.ds(ny * cut, width - ny * cut)], dst[1].at[here], out_sems.at[at + ny]
            )
        ]

    def send(src, at, mine, k):
        @pl.when(core == mine)
        def _():
            for copy in out_copies(src, keep, at, k):
                copy.start()

        @pl.when(core != mine)
        def _():
            for copy in out_copies(src, give, at, k):
                copy.start()

    wide = nt // 2 * depth
    for k in range(2):
        rows = image[pl.ds(k * nt // 2, nt // 2)].reshape(wide, ni)
        part_i[pl.ds(k * wide, wide)] = contract(rows, backs[...], (1, 0)).astype(BF)
    for k in range(full // step):
        send(part_i, 0, 0, k)

    for j in range(nj // TILE):
        here = pl.ds(j * TILE, TILE)
        grad = coef * contract(weight[:, here], unit_i[...], (0, 0))
        backs[here] = back(raw_t[here], grad)

    for k in range(full // step):
        here = pl.ds(k * step, step)
        part_t[here] = contract(texts[:, here], backs[...], (0, 0)).astype(BF)
        send(part_t, full // step * (ny + 1), 1, k)

    for k in range(full // step):
        for copy in out_copies(part_i, keep, 0, k):
            copy.wait()
        for copy in out_copies(part_t, give, full // step * (ny + 1), k):
            copy.wait()


def on_device(image_feat, text_feat, image_head, text_head, logit_scale, logit_bias):
    nz, ny = lax.axis_size("z"), lax.axis_size("yh")
    nt = lax.axis_size("yl") * lax.axis_size("x")
    pairs, depth = image_feat.shape
    width = image_head.shape[1]
    rows = pairs // nt
    full = nt * depth
    core = lax.axis_index("core")
    z = lax.axis_index("z")
    yh = lax.axis_index("yh")
    t = lax.axis_index(T)
    batch = pairs * nz * ny * 2
    coef = logit_scale[0] * (1.0 / math.sqrt(batch))

    nb = width // LANE
    low = -(-nb // 2)
    head = jnp.where(core == 0, image_head, text_head).reshape(depth, nb, LANE)
    head = jnp.where(yh == 0, head[:, :low], head[:, nb - low :]).transpose(1, 0, 2)
    columns = image_feat.T.reshape(depth, pairs // LANE, LANE).transpose(1, 0, 2)
    packed = jnp.concatenate([head, columns], axis=0)
    packed, text_feat = lax.optimization_barrier((packed, text_feat))
    packed = lax.all_gather(packed, PLANE, axis=0)

    split = text_feat.reshape(nt, rows, depth)
    own = lax.all_to_all(split, T, 0, 0, tiled=True).transpose(1, 0, 2).reshape(rows, full)
    text_a = spread(own, "z", nz).reshape(nz * rows, full)
    text_b = lax.ppermute(text_a, "core", SWAP)
    k = jnp.arange(nz * rows, dtype=jnp.int32)
    ids = jnp.concatenate(
        [((k // rows * ny + yh) * 2 + c) * pairs + t * rows + k % rows for c in (core, 1 - core)]
    )[None]
    info = jnp.stack([core] + [((z * ny + y) * 2 + core) * pairs for y in range(ny)])
    scalars = jnp.stack([logit_scale[0], logit_bias[0], coef])

    packed, text_a, text_b, ids, info, scalars = lax.optimization_barrier(
        (packed, text_a, text_b, ids, info, scalars)
    )
    other = lax.ppermute(packed[:, :low], "core", SWAP)

    ni, nj = ny * pairs, 2 * nz * rows
    smem = pl.BlockSpec(memory_space=pltpu.SMEM)
    vmem = pl.BlockSpec(memory_space=pltpu.VMEM)
    hbm = pl.BlockSpec(memory_space=pl.ANY)
    cut = width // LANE // 3 * LANE
    sums = [
        jax.ShapeDtypeStruct((ny, full, cut), BF),
        jax.ShapeDtypeStruct((full, width - ny * cut), BF),
    ]
    keep_a, keep_b, give_a, give_b, losses = pl.pallas_call(
        functools.partial(block_kernel, low),
        out_shape=[
            *sums,
            *sums,
            jax.ShapeDtypeStruct((1, ni), F32),
        ],
        in_specs=[smem, smem, vmem, hbm, hbm, hbm, hbm],
        out_specs=[hbm, hbm, hbm, hbm, vmem],
        scratch_shapes=[
            pltpu.VMEM((nt, depth, width), BF),
            pltpu.VMEM((nt, depth, width), BF),
            pltpu.VMEM((nt, depth, ni), BF),
            pltpu.VMEM((nj, full), BF),
            pltpu.VMEM((nj, width), F32),
            pltpu.VMEM((nj, width), BF),
            pltpu.VMEM((ni, width), BF),
            pltpu.VMEM((ni, nj), BF),
            pltpu.VMEM((max(ni, nj), width), BF),
            pltpu.VMEM((full, width), BF),
            pltpu.VMEM((full, width), BF),
            pltpu.SemaphoreType.DMA((2 * nb + 2 + ni // LANE,)),
            pltpu.SemaphoreType.DMA((2 * (full // (3 * LANE)) * (ny + 1),)),
        ],
        compiler_params=pltpu.CompilerParams(vmem_limit_bytes=LIMIT),
        cost_estimate=pl.CostEstimate(
            flops=4 * (ni + nj) * full * width + 6 * ni * nj * width,
            bytes_accessed=20 * 1024 * 1024,
            transcendentals=3 * ni * nj,
        ),
        name="block",
    )(info, scalars, ids, packed, other, text_a, text_b)

    nx, nyl = lax.axis_size("x"), lax.axis_size("yl")
    n_y = ny * nyl
    x = lax.axis_index("x")
    half = depth // 2

    def two_parts(loss):
        first = lax.reduce_precision(loss, 8, 7)
        parts = jnp.concatenate([first, loss - first], axis=-1).astype(BF)
        spare = 8 * cut - 2 * pairs
        parts = jnp.pad(parts, [(0, 0)] * (parts.ndim - 1) + [(0, spare)])
        return parts.reshape(parts.shape[:-1] + (8, cut))

    def one_part(rows):
        return jnp.sum(rows.reshape(8 * cut)[: 2 * pairs].reshape(2, pairs), axis=0)

    def over(axes, n, at, chunk):
        total = chunk(at).astype(F32)
        for k in range(1, n):
            part = chunk(lax.rem(at + k, n)).astype(BF)
            part = lax.ppermute(part, axes, [(i, (i + k) % n) for i in range(n)])
            total = total + part.astype(F32)
        return total

    def core_sum(mine, other):
        return (mine.astype(F32) + lax.ppermute(other, "core", SWAP).astype(F32)).astype(BF)

    a = core_sum(keep_a, give_a).reshape(ny, nyl, nx * depth, cut)
    row = jnp.broadcast_to(two_parts(losses.reshape(ny, pairs))[:, None], (ny, nyl, 8, cut))
    a = jnp.concatenate([a, row], axis=2).reshape(n_y, nx * depth + 8, cut)
    a = lax.all_to_all(a, ("yh", "yl"), 0, 0, tiled=True)
    b = core_sum(keep_b, give_b).reshape(nyl, nx, depth, width - ny * cut)
    b = over("x", nx, x, lambda k: lax.dynamic_index_in_dim(b, k, 1, keepdims=False)).astype(BF)
    b = b.reshape(nyl, ny, half, width - ny * cut).transpose(1, 0, 2, 3).reshape(n_y, half, -1)
    at_y = lax.axis_index(("yh", "yl"))
    b = over(("yh", "yl"), n_y, at_y, lambda k: lax.dynamic_index_in_dim(b, k, 0, keepdims=False))

    a = jnp.sum(a.astype(F32), axis=0)
    row = two_parts(one_part(a[nx * depth :])).astype(F32)
    a = a[: nx * depth].reshape(nx, depth, cut)
    a = over(
        "x", nx, x, lambda k: jnp.concatenate([lax.dynamic_index_in_dim(a, k, 0, keepdims=False), row], axis=0)
    )
    row_loss = one_part(a[depth:]) / batch
    a = a[:depth].astype(BF)
    b = b.astype(BF)

    def to_tiles(v):
        r, c = v.shape
        return v.reshape(r // 8, 8, c // LANE, LANE).transpose(0, 2, 1, 3).reshape(-1, 8, LANE)

    def from_tiles(v, r, c):
        return v.reshape(r // 8, c // LANE, 8, LANE).transpose(0, 2, 1, 3).reshape(r, c)

    tiles_a = depth // 8 * (cut // LANE)
    one = jnp.concatenate([to_tiles(a), to_tiles(b)], axis=0)
    tiles = one.shape[0]
    per = -(-tiles // nz)
    one = jnp.pad(one, ((0, per * nz - tiles), (0, 0), (0, 0)))
    one = lax.all_to_all(one.reshape(nz, per * 8, LANE), "z", 0, 0, tiled=True)
    one = jnp.sum(one.astype(F32), axis=0).astype(BF)
    one = spread(one, ZY, nz * ny).reshape(nz, ny, per * 8, LANE).transpose(1, 0, 2, 3)
    one = one.reshape(ny, per * nz, 8, LANE)
    left = [from_tiles(one[y, :tiles_a], depth, cut) for y in range(ny)]
    right = [from_tiles(one[y, tiles_a:tiles], half, width - ny * cut) for y in range(ny)]
    one = jnp.concatenate([*left, jnp.concatenate(right, axis=0)], axis=1)
    two = lax.ppermute(one, "core", SWAP)
    out_i = jnp.where(core == 0, one, two).astype(F32)
    out_t = jnp.where(core == 0, two, one).astype(F32)
    return out_i, out_t, row_loss


def solution(mesh):
    fine = Mesh(mesh.devices.reshape(8, 2, 2, 2, 4), ("z", "yh", "core", "yl", "x"))
    dp = ("z", "yh", "core")
    placed = (P(dp, T), P(dp, T), P(T, None), P(T, None), P(), P())
    return jax.shard_map(
        on_device,
        mesh=fine,
        in_specs=placed,
        out_specs=(P(T, None), P(T, None), P(dp)),
        check_vma=False,
    )
```

```python
import functools
import math

import jax
import jax.numpy as jnp
from jax import lax
from jax.experimental import pallas as pl
from jax.experimental.pallas import tpu as pltpu
from jax.sharding import Mesh, PartitionSpec as P

BF = jnp.bfloat16
F32 = jnp.float32
T = ("yl", "x")
PLANE = ("yh", "yl", "x")
ZY = ("z", "yh")
SWAP = [(0, 1), (1, 0)]
LANE = 128
TILE = 512
LIMIT = 58 * 1024 * 1024


def spread(x, axes, n):
    wide = jnp.broadcast_to(x[None], (n,) + x.shape)
    return lax.all_to_all(wide, axes, 0, 0, tiled=True)


def contract(left, right, dims):
    return lax.dot_general(left, right, ((dims[:1], dims[1:]), ((), ())), preferred_element_type=F32)


def stats(raw):
    width = raw.shape[-1]
    mean_sq = jnp.mean(raw * raw, axis=-1, keepdims=True)
    return lax.rsqrt(mean_sq + 1e-06) * (1.0 / math.sqrt(width)), 1.0 / (width * (mean_sq + 1e-06))


def back(raw, grad):
    factor, inv = stats(raw)
    inner = jnp.sum(grad * raw, axis=-1, keepdims=True)
    return (factor * (grad - raw * (inner * inv))).astype(BF)


def head_copies(src, dst, sems, first):
    nt, nb = dst.shape[0], dst.shape[2] // LANE
    low = src.shape[1] if first is None else first
    out = []
    for b in range(nb):
        y, s = (0, b) if b < low else (1, b - nb + low)
        out.append(
            pltpu.make_async_copy(
                src.at[pl.ds(y * nt, nt), s], dst.at[:, :, pl.ds(b * LANE, LANE)], sems.at[b]
            )
        )
    return out


def block_kernel(
    low, info, scalars, ids, packed, other, text_a, text_b,
    keep_a, keep_b, give_a, give_b, loss,
    head_i, head_t, image, texts, raw_t, unit_t, unit_i, weight, backs, part_i, part_t, sems, out_sems,
):
    nt, depth, width = head_i.shape
    full = nt * depth
    ni, nj = image.shape[2], texts.shape[0]
    core = info[0]
    scale, bias, coef = scalars[0], scalars[1], scalars[2]

    nb = width // LANE
    text_copies = [
        pltpu.make_async_copy(text_a, texts.at[pl.ds(0, nj // 2)], sems.at[2 * nb]),
        pltpu.make_async_copy(text_b, texts.at[pl.ds(nj // 2, nj // 2)], sems.at[2 * nb + 1]),
    ]
    half = ni // LANE // 2
    image_copies = [
        pltpu.make_async_copy(
            packed.at[pl.ds((b // half) * nt, nt), low + b % half],
            image.at[:, :, pl.ds(b * LANE, LANE)],
            sems.at[2 * nb + 2 + b],
        )
        for b in range(2 * half)
    ]
    sems_i, sems_t = sems.at[pl.ds(0, nb)], sems.at[pl.ds(nb, nb)]

    def start_head(dst, at, mine):
        @pl.when(core == mine)
        def _():
            for copy in head_copies(packed, dst, at, low):
                copy.start()

        @pl.when(core != mine)
        def _():
            for copy in head_copies(other, dst, at, low):
                copy.start()

    text_copies[0].start()
    start_head(head_t, sems_t, 1)
    for copy in text_copies[:1] + head_copies(packed, head_t, sems_t, low):
        copy.wait()
    text_copies[1].start()
    start_head(head_i, sems_i, 0)
    for copy in image_copies:
        copy.start()

    for j in range(nj // TILE):
        if j * TILE == nj // 2:
            text_copies[1].wait()
        here = pl.ds(j * TILE, TILE)
        raw = contract(texts[here], head_t[...].reshape(full, width), (1, 0))
        raw_t[here] = raw
        unit_t[here] = (raw * stats(raw)[0]).astype(BF)

    for copy in head_copies(packed, head_i, sems_i, low) + image_copies:
        copy.wait()

    for i in range(ni // TILE):
        here = pl.ds(i * TILE, TILE)
        tile = image[:, :, here].reshape(full, TILE)
        raw = contract(tile, head_i[...].reshape(full, width), (0, 0))
        unit = (raw * stats(raw)[0]).astype(BF)
        unit_i[here] = unit
        scores = scale * contract(unit, unit_t[...], (1, 1)) + bias
        per = ni // 2 // TILE
        base = info[1 + i // per] + i % per * TILE
        rows = base + lax.broadcasted_iota(jnp.int32, (TILE, 1), 0)
        match = rows == ids[...]
        small = jnp.exp(-jnp.abs(scores))
        soft = jnp.maximum(scores, 0.0) + jnp.log1p(small)
        sig = jnp.where(scores >= 0.0, 1.0, small) / (1.0 + small)
        terms = soft - jnp.where(match, scores, 0.0)
        total = terms[:, :LANE]
        for b in range(1, nj // LANE):
            total = total + terms[:, b * LANE : (b + 1) * LANE]
        loss[:, here] = jnp.sum(total.T, axis=0, keepdims=True)
        grads = jnp.where(match, sig - 1.0, sig).astype(BF)
        weight[here] = grads
        grad = coef * contract(grads, unit_t[...], (1, 0))
        backs[here] = back(raw, grad)

    step = 3 * LANE

    keep, give = (keep_a, keep_b), (give_a, give_b)
    ny, _, cut = keep_a.shape

    def out_copies(src, dst, at, k):
        here = pl.ds(k * step, step)
        at = at + k * (ny + 1)
        return [
            pltpu.make_async_copy(
                src.at[here, pl.ds(y * cut, cut)], dst[0].at[y, here], out_sems.at[at + y]
            )
            for y in range(ny)
        ] + [
            pltpu.make_async_copy(
                src.at[here, pl.ds(ny * cut, width - ny * cut)], dst[1].at[here], out_sems.at[at + ny]
            )
        ]

    def send(src, at, mine, k):
        @pl.when(core == mine)
        def _():
            for copy in out_copies(src, keep, at, k):
                copy.start()

        @pl.when(core != mine)
        def _():
            for copy in out_copies(src, give, at, k):
                copy.start()

    wide = nt // 2 * depth
    for k in range(2):
        rows = image[pl.ds(k * nt // 2, nt // 2)].reshape(wide, ni)
        part_i[pl.ds(k * wide, wide)] = contract(rows, backs[...], (1, 0)).astype(BF)
    for k in range(full // step):
        send(part_i, 0, 0, k)

    for j in range(nj // TILE):
        here = pl.ds(j * TILE, TILE)
        grad = coef * contract(weight[:, here], unit_i[...], (0, 0))
        backs[here] = back(raw_t[here], grad)

    for k in range(full // step):
        here = pl.ds(k * step, step)
        part_t[here] = contract(texts[:, here], backs[...], (0, 0)).astype(BF)
        send(part_t, full // step * (ny + 1), 1, k)

    for k in range(full // step):
        for copy in out_copies(part_i, keep, 0, k):
            copy.wait()
        for copy in out_copies(part_t, give, full // step * (ny + 1), k):
            copy.wait()


def on_device(image_feat, text_feat, image_head, text_head, logit_scale, logit_bias):
    nz, ny = lax.axis_size("z"), lax.axis_size("yh")
    nt = lax.axis_size("yl") * lax.axis_size("x")
    pairs, depth = image_feat.shape
    width = image_head.shape[1]
    rows = pairs // nt
    full = nt * depth
    core = lax.axis_index("core")
    z = lax.axis_index("z")
    yh = lax.axis_index("yh")
    t = lax.axis_index(T)
    batch = pairs * nz * ny * 2
    coef = logit_scale[0] * (1.0 / math.sqrt(batch))

    nb = width // LANE
    low = -(-nb // 2)
    head = jnp.where(core == 0, image_head, text_head).reshape(depth, nb, LANE)
    head = jnp.where(yh == 0, head[:, :low], head[:, nb - low :]).transpose(1, 0, 2)
    columns = image_feat.T.reshape(depth, pairs // LANE, LANE).transpose(1, 0, 2)
    packed = jnp.concatenate([head, columns], axis=0)
    packed, text_feat = lax.optimization_barrier((packed, text_feat))
    packed = lax.all_gather(packed, PLANE, axis=0)

    split = text_feat.reshape(nt, rows, depth)
    own = lax.all_to_all(split, T, 0, 0, tiled=True).transpose(1, 0, 2).reshape(rows, full)
    text_a = spread(own, "z", nz).reshape(nz * rows, full)
    text_b = lax.ppermute(text_a, "core", SWAP)
    k = jnp.arange(nz * rows, dtype=jnp.int32)
    ids = jnp.concatenate(
        [((k // rows * ny + yh) * 2 + c) * pairs + t * rows + k % rows for c in (core, 1 - core)]
    )[None]
    info = jnp.stack([core] + [((z * ny + y) * 2 + core) * pairs for y in range(ny)])
    scalars = jnp.stack([logit_scale[0], logit_bias[0], coef])

    packed, text_a, text_b, ids, info, scalars = lax.optimization_barrier(
        (packed, text_a, text_b, ids, info, scalars)
    )
    other = lax.ppermute(packed[:, :low], "core", SWAP)

    ni, nj = ny * pairs, 2 * nz * rows
    smem = pl.BlockSpec(memory_space=pltpu.SMEM)
    vmem = pl.BlockSpec(memory_space=pltpu.VMEM)
    hbm = pl.BlockSpec(memory_space=pl.ANY)
    cut = width // LANE // 4 * LANE
    sums = [
        jax.ShapeDtypeStruct((ny, full, cut), BF),
        jax.ShapeDtypeStruct((full, width - ny * cut), BF),
    ]
    keep_a, keep_b, give_a, give_b, losses = pl.pallas_call(
        functools.partial(block_kernel, low),
        out_shape=[
            *sums,
            *sums,
            jax.ShapeDtypeStruct((1, ni), F32),
        ],
        in_specs=[smem, smem, vmem, hbm, hbm, hbm, hbm],
        out_specs=[hbm, hbm, hbm, hbm, vmem],
        scratch_shapes=[
            pltpu.VMEM((nt, depth, width), BF),
            pltpu.VMEM((nt, depth, width), BF),
            pltpu.VMEM((nt, depth, ni), BF),
            pltpu.VMEM((nj, full), BF),
            pltpu.VMEM((nj, width), F32),
            pltpu.VMEM((nj, width), BF),
            pltpu.VMEM((ni, width), BF),
            pltpu.VMEM((ni, nj), BF),
            pltpu.VMEM((max(ni, nj), width), BF),
            pltpu.VMEM((full, width), BF),
            pltpu.VMEM((full, width), BF),
            pltpu.SemaphoreType.DMA((2 * nb + 2 + ni // LANE,)),
            pltpu.SemaphoreType.DMA((2 * (full // (3 * LANE)) * (ny + 1),)),
        ],
        compiler_params=pltpu.CompilerParams(vmem_limit_bytes=LIMIT),
        cost_estimate=pl.CostEstimate(
            flops=4 * (ni + nj) * full * width + 6 * ni * nj * width,
            bytes_accessed=20 * 1024 * 1024,
            transcendentals=3 * ni * nj,
        ),
        name="block",
    )(info, scalars, ids, packed, other, text_a, text_b)

    nx, nyl = lax.axis_size("x"), lax.axis_size("yl")
    n_y = ny * nyl
    x = lax.axis_index("x")
    half = depth // 2

    def two_parts(loss):
        first = lax.reduce_precision(loss, 8, 7)
        parts = jnp.concatenate([first, loss - first], axis=-1).astype(BF)
        spare = 8 * cut - 2 * pairs
        parts = jnp.pad(parts, [(0, 0)] * (parts.ndim - 1) + [(0, spare)])
        return parts.reshape(parts.shape[:-1] + (8, cut))

    def one_part(rows):
        return jnp.sum(rows.reshape(8 * cut)[: 2 * pairs].reshape(2, pairs), axis=0)

    def over(axes, n, at, chunk):
        total = chunk(at).astype(F32)
        for k in range(1, n):
            part = chunk(lax.rem(at + k, n)).astype(BF)
            part = lax.ppermute(part, axes, [(i, (i + k) % n) for i in range(n)])
            total = total + part.astype(F32)
        return total

    def core_sum(mine, other):
        return (mine.astype(F32) + lax.ppermute(other, "core", SWAP).astype(F32)).astype(BF)

    a = core_sum(keep_a, give_a).reshape(ny, nyl, nx * depth, cut)
    row = jnp.broadcast_to(two_parts(losses.reshape(ny, pairs))[:, None], (ny, nyl, 8, cut))
    a = jnp.concatenate([a, row], axis=2).reshape(n_y, nx * depth + 8, cut)
    a = lax.all_to_all(a, ("yh", "yl"), 0, 0, tiled=True)
    b = core_sum(keep_b, give_b).reshape(nyl, nx, depth, width - ny * cut)
    b = over("x", nx, x, lambda k: lax.dynamic_index_in_dim(b, k, 1, keepdims=False)).astype(BF)
    b = b.reshape(nyl, ny, half, width - ny * cut).transpose(1, 0, 2, 3).reshape(n_y, half, -1)
    at_y = lax.axis_index(("yh", "yl"))
    b = over(("yh", "yl"), n_y, at_y, lambda k: lax.dynamic_index_in_dim(b, k, 0, keepdims=False))

    a = jnp.sum(a.astype(F32), axis=0)
    row = two_parts(one_part(a[nx * depth :])).astype(F32)
    a = a[: nx * depth].reshape(nx, depth, cut)
    a = over(
        "x", nx, x, lambda k: jnp.concatenate([lax.dynamic_index_in_dim(a, k, 0, keepdims=False), row], axis=0)
    )
    row_loss = one_part(a[depth:]) / batch
    a = a[:depth].astype(BF)
    b = b.astype(BF)

    def to_tiles(v):
        r, c = v.shape
        return v.reshape(r // 8, 8, c // LANE, LANE).transpose(0, 2, 1, 3).reshape(-1, 8, LANE)

    def from_tiles(v, r, c):
        return v.reshape(r // 8, c // LANE, 8, LANE).transpose(0, 2, 1, 3).reshape(r, c)

    tiles_a = depth // 8 * (cut // LANE)
    one = jnp.concatenate([to_tiles(a), to_tiles(b)], axis=0)
    tiles = one.shape[0]
    per = -(-tiles // nz)
    one = jnp.pad(one, ((0, per * nz - tiles), (0, 0), (0, 0)))
    one = lax.all_to_all(one.reshape(nz, per * 8, LANE), "z", 0, 0, tiled=True)
    one = jnp.sum(one.astype(F32), axis=0).astype(BF)
    one = spread(one, ZY, nz * ny).reshape(nz, ny, per * 8, LANE).transpose(1, 0, 2, 3)
    one = one.reshape(ny, per * nz, 8, LANE)
    left = [from_tiles(one[y, :tiles_a], depth, cut) for y in range(ny)]
    right = [from_tiles(one[y, tiles_a:tiles], half, width - ny * cut) for y in range(ny)]
    one = jnp.concatenate([*left, jnp.concatenate(right, axis=0)], axis=1)
    two = lax.ppermute(one, "core", SWAP)
    out_i = jnp.where(core == 0, one, two).astype(F32)
    out_t = jnp.where(core == 0, two, one).astype(F32)
    return out_i, out_t, row_loss


def solution(mesh):
    fine = Mesh(mesh.devices.reshape(8, 2, 2, 2, 4), ("z", "yh", "core", "yl", "x"))
    dp = ("z", "yh", "core")
    placed = (P(dp, T), P(dp, T), P(T, None), P(T, None), P(), P())
    return jax.shard_map(
        on_device,
        mesh=fine,
        in_specs=placed,
        out_specs=(P(T, None), P(T, None), P(dp)),
        check_vma=False,
    )
```
